32 devices in a mesh: graph: 16 (over z, y, x), rep: 2 (over core).
Axes of the slice: x: 2, y: 2, z: 4, core: 2. Of those that a mesh axis runs over, the one named last changes fastest.
Arguments:
- grad_out: bfloat16 [8192, 256], P(('graph', 'rep')), may hold values from -6 to 6
- pre_act: bfloat16 [8192, 256], P(('graph', 'rep')), may hold values from -6 to 6
- aggregated: bfloat16 [8192, 256], P(('graph', 'rep')), may hold values from -0.3125 to 0.3125
- weight: bfloat16 [256, 256], replicated, may hold values from -0.375 to 0.375
- adj_tiles: bfloat16 [16, 2, 16, 2, 128, 128], P('graph', 'rep'), may hold values from 0 to 0.039794922
- tile_row: int32 [16, 2, 16, 2], P('graph', 'rep'), may hold values from 0 to 1
- tile_col: int32 [16, 2, 16, 2], P('graph', 'rep'), may hold values from 0 to 3
- tile_count: int32 [16, 2, 16], P('graph', 'rep'), may hold values from 0 to 2, as said below
- node_perm: int32 [16, 512], P('graph'), may hold values from 0 to 511, each once within a row
Outputs:
- input_grad: bfloat16 [8192, 256], P(('graph', 'rep'))
- weight_grad: float32 [256, 256], replicated
- relu_grad: bfloat16 [8192, 256], P(('graph', 'rep'))
The draws below stay inside these ranges and needn't reach their ends.
Inputs may be any that keep to these rules, and one draw needn't show every extreme that they name: tile_count[g, r, g] is 2 for every partition g and replica r. `node_perm`: each row is a permutation.
All inputs are finite; a program needn't handle non-finite values.
Results may differ from the reference program's by a relative error of at most 0.0049.
Values may be sent and summed in bfloat16 or wider, within the bound.
A program may use at most 128 MiB of HBM per device.

```python
import jax
import jax.numpy as jnp
from jax import lax

WIDTH = 256
TILE = 128
ROW_BLOCKS = 2
SLOTS = 2
PARTS_SIZE = 16
REPS = 2
PART_ROWS = 512
COL_BLOCKS = 4
NODES = 8192


def draw_tile_count(key, part):
    key_base, key_load = jax.random.split(key)
    draws_base = jax.random.randint(key_base, (PARTS_SIZE, REPS, PARTS_SIZE), 0, 4)
    load_shift = jax.random.randint(key_load, (PARTS_SIZE, REPS, 1), 0, 4)
    filled = jnp.clip(draws_base + load_shift - 2, 0, SLOTS)
    own_part = jnp.arange(PARTS_SIZE)[:, None, None] == jnp.arange(PARTS_SIZE)[None, None, :]
    return jnp.where(own_part, SLOTS, filled).astype(jnp.int32)


def with_ends(entries, key, least, largest):
    longest = entries.shape.index(max(entries.shape))
    spots = []
    for shift in (0, 1):
        where = [jax.random.randint(jax.random.fold_in(key, axis), (), 0, length) for axis, length in enumerate(entries.shape)]
        where[longest] = (where[longest] + shift) % entries.shape[longest]
        spots.append(tuple(where))
    return entries.at[spots[0]].set(least).at[spots[1]].set(largest)


def block_levels(rng, dims, pieces, low, largest):
    level, own = 1.0, jax.random.fold_in(rng, 6)
    for position, parts in pieces:
        heights = jnp.exp(jax.random.uniform(jax.random.fold_in(own, position), (parts,), jnp.float32, low / len(pieces), largest / len(pieces)))
        level = level * jnp.repeat(heights, dims[position] // parts).reshape([-1 if axis == position else 1 for axis in range(len(dims))])
    return level


def centred(key, dims, deviation, most, cuts=(), dtype=jnp.bfloat16):
    factor_of = block_levels(key, dims, cuts, -0.22, 0.18) if cuts else 1.0
    result = jax.random.normal(key, dims, jnp.float32) * deviation * factor_of
    return jnp.minimum(jnp.maximum(result, -most), most).astype(dtype)


def setup_inputs(seed: int = 0) -> dict:
    streams_of = jax.random.split(jax.random.key(seed), 10)
    grad_out = centred(streams_of[0], (NODES, WIDTH), 1.0, 6.0, ((0, 32),))
    pre_act = centred(streams_of[1], (NODES, WIDTH), 1.0, 6.0, ((0, 32),))
    aggregated = centred(streams_of[2], (NODES, WIDTH), (2.0 / NODES ** 0.5), 0.3125, ((0, 32),))
    weight = centred(streams_of[3], (WIDTH, WIDTH), WIDTH ** -0.5, 0.375)
    adj_tiles = jnp.clip(0.039794922 * jax.random.uniform(streams_of[4], (PARTS_SIZE, REPS, PARTS_SIZE, SLOTS, TILE, TILE), jnp.float32) ** block_levels(streams_of[4], (PARTS_SIZE, REPS, PARTS_SIZE, SLOTS, TILE, TILE), ((0, 16), (1, 2)), -0.2, 0.2), 0.0, 0.039794922).astype(jnp.bfloat16)
    tile_row = with_ends(jax.random.randint(streams_of[5], (PARTS_SIZE, REPS, PARTS_SIZE, SLOTS), 0, ROW_BLOCKS), jax.random.fold_in(streams_of[5], 1), 0, ROW_BLOCKS - 1).astype(jnp.int32)
    tile_col = with_ends(jax.random.randint(streams_of[6], (PARTS_SIZE, REPS, PARTS_SIZE, SLOTS), 0, COL_BLOCKS), jax.random.fold_in(streams_of[6], 1), 0, COL_BLOCKS - 1).astype(jnp.int32)
    tile_count = draw_tile_count(jax.random.fold_in(streams_of[9], 71), 0)
    node_perm = jax.vmap(lambda own: jax.random.permutation(own, PART_ROWS))(jax.random.split(streams_of[8], PARTS_SIZE)).reshape((PARTS_SIZE, PART_ROWS)).astype(jnp.int32)
    return {"grad_out": grad_out, "pre_act": pre_act, "aggregated": aggregated, "weight": weight, "adj_tiles": adj_tiles, "tile_row": tile_row, "tile_col": tile_col, "tile_count": tile_count, "node_perm": node_perm}


def reference(grad_out, pre_act, aggregated, weight, adj_tiles, tile_row, tile_col, tile_count, node_perm):
    relu_grad = jnp.where(pre_act > 0, grad_out, jnp.zeros_like(grad_out))
    weight_grad = jnp.dot(aggregated.T, relu_grad, preferred_element_type=jnp.float32)
    back_agg = jnp.dot(relu_grad, weight.T, preferred_element_type=jnp.float32).astype(jnp.bfloat16)
    back_blocks = back_agg.reshape(PARTS_SIZE, REPS, ROW_BLOCKS, TILE, WIDTH)
    part_axis = jnp.arange(PARTS_SIZE)[:, None]
    slot_axis = jnp.arange(SLOTS)[None, :]
    column_axis = jnp.arange(COL_BLOCKS)

    def partition_grad(group_index):
        running = jnp.zeros((COL_BLOCKS, TILE, WIDTH), jnp.float32)
        for replica in range(REPS):
            sources = back_blocks[:, replica]
            chosen = sources[part_axis, tile_row[group_index, replica]]
            product = jnp.einsum('psab,psac->psbc', adj_tiles[group_index, replica].astype(jnp.float32), chosen.astype(jnp.float32))
            alive = (slot_axis < tile_count[group_index, replica][:, None]).astype(jnp.float32)
            select = (tile_col[group_index, replica][:, :, None] == column_axis[None, None, :]).astype(jnp.float32) * alive[:, :, None]
            running = running + jnp.einsum('psd,psbc->dbc', select, product, precision=lax.Precision.HIGHEST)
        flat_grad = running.reshape(PART_ROWS, WIDTH)
        return flat_grad[node_perm[group_index]]
    node_rows = lax.map(partition_grad, jnp.arange(PARTS_SIZE))
    input_grad = node_rows.reshape(NODES, WIDTH).astype(jnp.bfloat16)
    return (input_grad, weight_grad, relu_grad)
```

```python
import functools

import jax
import jax.numpy as jnp
from jax import lax
from jax.experimental import pallas as pl
from jax.experimental.pallas import tpu as pltpu
from jax.sharding import PartitionSpec as P

MESH = pl.DeviceIdType.MESH
BF16 = jnp.bfloat16
F32 = jnp.float32
LINE = 4
PLANE = 4


def nearest(z, k):
    if k == 0:
        return z
    low = jnp.where(z < 2, z, 3 - z)
    value = (1 - low) if k == 1 else k
    return jnp.where(z < 2, value, 3 - value)


def fused(
    grad_ref, pre_ref, agg_ref, weight_ref, tiles_hbm, row_ref, col_ref, count_ref, perm_ref,
    input_ref, wgrad_ref, relu_ref,
    blocks, tiles, folded, perm_wide, total, outgoing, incoming,
    w_part, w_pair, w_mine, w_parts, w_done, w_other,
    tile_sem, send_sem, recv_sem, diag_send, diag_recv, w_send, w_recv, pair_send, pair_recv,
):
    parts, rows, width = blocks.shape
    tile = tiles.shape[-1]
    g = lax.axis_index("graph")
    r = lax.axis_index("rep")
    other = 1 - r
    z = g // PLANE
    spot = g - z * PLANE
    y = spot // 2
    x = spot - y * 2
    across_y = (1 - y) * 2 + x
    across_x = y * 2 + (1 - x)
    across_xy = (1 - y) * 2 + (1 - x)

    def peer(k):
        return lax.rem(g + k, parts)

    barrier = pltpu.get_barrier_semaphore()

    def greet(k, carry):
        pl.semaphore_signal(barrier, inc=1, device_id=(peer(k), r), device_id_type=MESH)
        return carry

    lax.fori_loop(1, parts, greet, 0)
    pl.semaphore_signal(barrier, inc=1, device_id=(g, other), device_id_type=MESH)

    load_tiles = pltpu.make_async_copy(tiles_hbm, tiles, tile_sem)
    load_tiles.start()

    grad = grad_ref[...]
    relu_ref[...] = jnp.where(pre_ref[...] > 0, grad, jnp.zeros_like(grad))
    blocks[g] = lax.dot_general(
        relu_ref[...], weight_ref[...], (((1,), (1,)), ((), ())), preferred_element_type=F32
    ).astype(BF16)

    def whole(origin, target, slot, way):
        return pltpu.make_async_remote_copy(
            src_ref=blocks.at[origin],
            dst_ref=blocks.at[origin],
            send_sem=send_sem.at[slot, way],
            recv_sem=recv_sem.at[origin],
            device_id=(target, r),
            device_id_type=MESH,
        )

    def half(k, via):
        zz = nearest(z, k)
        from_here = zz * PLANE + (across_y if via == 0 else across_x)
        part = pl.ds(via * tile, tile)
        return pltpu.make_async_remote_copy(
            src_ref=blocks.at[from_here, part],
            dst_ref=blocks.at[from_here, part],
            send_sem=diag_send.at[via, k],
            recv_sem=diag_recv.at[via, zz],
            device_id=(z * PLANE + (across_x if via == 0 else across_y), r),
            device_id_type=MESH,
        )

    def half_in(k, via):
        zz = nearest(z, k)
        origin = zz * PLANE + across_xy
        part = pl.ds(via * tile, tile)
        return pltpu.make_async_remote_copy(
            src_ref=blocks.at[origin, part],
            dst_ref=blocks.at[origin, part],
            send_sem=diag_send.at[via, k],
            recv_sem=diag_recv.at[via, zz],
            device_id=(z * PLANE + (across_x if via == 0 else across_y), r),
            device_id_type=MESH,
        )

    def along_z(k, act):
        zz = nearest(z, k)
        origin = zz * PLANE + spot
        if k == 0:
            @pl.when(z < LINE - 1)
            def _():
                act(whole(origin, g + PLANE, k, 0))

            @pl.when(z > 0)
            def _():
                act(whole(origin, g - PLANE, k, 1))
        else:
            @pl.when((zz < z) & (z < LINE - 1))
            def _():
                act(whole(origin, g + PLANE, k, 0))

            @pl.when((zz > z) & (z > 0))
            def _():
                act(whole(origin, g - PLANE, k, 1))

    def in_plane(k, act):
        origin = nearest(z, k) * PLANE + spot
        act(whole(origin, z * PLANE + across_y, k, 2))
        act(whole(origin, z * PLANE + across_x, k, 3))

    def start(copy):
        copy.start()

    def wait_sent(copy):
        copy.wait_send()

    def received(origin):
        whole(origin, z * PLANE + across_y, 0, 2).wait_recv()

    def spread(k):
        if k > 0:
            received(nearest(z, k) * PLANE + spot)
        along_z(k, start)
        in_plane(k, start)

    def turn(k):
        zz = nearest(z, k)
        received(zz * PLANE + across_y)
        half(k, 0).start()
        received(zz * PLANE + across_x)
        half(k, 1).start()

    def fold(first, many):
        lanes = lax.broadcasted_iota(jnp.int32, perm_wide.shape, 1)

        def one(p, carry):
            for s in range(2):
                base = jnp.where(count_ref[0, p] > s, col_ref[s, p] * tile, -4 * parts * rows)
                hot = jnp.where(perm_wide[...] == lanes + base, 1.0, 0.0).astype(BF16)
                folded[p, :, s * tile : (s + 1) * tile] = lax.dot_general(
                    hot, tiles[p, s], (((1,), (1,)), ((), ())), preferred_element_type=F32
                ).astype(BF16)
            return carry

        lax.fori_loop(first, first + many, one, 0)

    def chosen(p):
        top = blocks[p, :tile, :]
        low = blocks[p, tile:, :]
        return jnp.concatenate([jnp.where(row_ref[s, p] == 0, top, low) for s in range(2)], axis=0)

    def product(p, side, source):
        return jnp.dot(
            folded[p, pl.ds(side * rows, rows), :], source, preferred_element_type=F32
        )

    def add(p, first=False):
        source = chosen(p)
        for side in range(2):
            if first:
                total[side] = product(p, side, source)
            else:
                total[side] += product(p, side, source)

    def pair(src, dst, which):
        return pltpu.make_async_remote_copy(
            src_ref=src,
            dst_ref=dst,
            send_sem=pair_send.at[which],
            recv_sem=pair_recv.at[which],
            device_id=(g, other),
            device_id_type=MESH,
        )

    def scatter_w(k):
        to = peer(k)
        return pltpu.make_async_remote_copy(
            src_ref=w_mine.at[to],
            dst_ref=w_parts.at[g],
            send_sem=w_send.at[0, k],
            recv_sem=w_recv.at[0, g],
            device_id=(to, r),
            device_id_type=MESH,
        )

    def gather_w(k):
        return pltpu.make_async_remote_copy(
            src_ref=w_done.at[g],
            dst_ref=w_done.at[g],
            send_sem=w_send.at[1, k],
            recv_sem=w_recv.at[1, g],
            device_id=(peer(k), r),
            device_id_type=MESH,
        )

    def wait_w(phase, buffer):
        def one(k, carry):
            origin = peer(k)
            pltpu.make_async_remote_copy(
                src_ref=buffer.at[origin],
                dst_ref=buffer.at[origin],
                send_sem=w_send.at[phase, k],
                recv_sem=w_recv.at[phase, origin],
                device_id=(origin, r),
                device_id_type=MESH,
            ).wait_recv()
            return carry

        lax.fori_loop(1, parts, one, 0)

    def each_peer(make, act):
        def one(k, carry):
            act(make(k))
            return carry

        lax.fori_loop(1, parts, one, 0)

    pl.semaphore_wait(barrier, parts)
    spread(0)

    w_part[...] = lax.dot_general(
        agg_ref[...], relu_ref[...], (((0,), (0,)), ((), ())), preferred_element_type=F32
    ).reshape(w_part.shape)
    w_swap = pair(w_part.at[other], w_pair, 0)
    w_swap.start()

    perm_wide[...] = jnp.broadcast_to(perm_ref[...], (tile, perm_wide.shape[0])).T
    load_tiles.wait()
    fold(0, 2)
    spread(1)

    w_swap.wait_recv()
    w_mine[...] = w_part[r] + w_pair[...]
    each_peer(scatter_w, start)
    w_parts[g] = w_mine[g]
    turn(0)
    fold(2, 4)
    spread(2)
    turn(1)
    wait_w(0, w_parts)
    w_done[g] = jnp.sum(w_parts[...], axis=0)
    each_peer(gather_w, start)
    fold(6, 4)
    spread(3)
    turn(2)
    fold(10, 6)
    turn(3)
    wait_w(1, w_done)
    w_back = pair(w_done, w_other, 1)
    w_back.start()

    add(g, first=True)
    for k in range(1, LINE):
        add(nearest(z, k) * PLANE + spot)
    for k in range(LINE):
        add(nearest(z, k) * PLANE + across_y)
        add(nearest(z, k) * PLANE + across_x)

    w_back.wait_recv()
    w_rows = width // 2
    wgrad_ref[pl.ds(pl.multiple_of(r * w_rows, w_rows), w_rows), :] = w_done[...].reshape(w_rows, width)
    wgrad_ref[pl.ds(pl.multiple_of(other * w_rows, w_rows), w_rows), :] = w_other[...].reshape(w_rows, width)

    for k in range(LINE):
        half_in(k, 0).wait_recv()
        half_in(k, 1).wait_recv()
        p = nearest(z, k) * PLANE + across_xy
        if k < LINE - 1:
            add(p)
    source = chosen(p)
    outgoing[...] = total[other] + product(p, other, source)
    swap = pair(outgoing, incoming, 2)
    swap.start()
    total[r] += product(p, r, source)

    for k in range(LINE):
        along_z(k, wait_sent)
        in_plane(k, wait_sent)
        half(k, 0).wait_send()
        half(k, 1).wait_send()
    each_peer(scatter_w, wait_sent)
    each_peer(gather_w, wait_sent)
    w_swap.wait_send()
    w_back.wait_send()
    swap.wait_recv()
    input_ref[...] = (total[r] + incoming[...]).astype(BF16)
    swap.wait_send()


def fused_body(
    grad_out, pre_act, aggregated, weight, adj_tiles, tile_row, tile_col, tile_count, node_perm
):
    rows, width = grad_out.shape
    parts, slots, tile = adj_tiles.shape[2], adj_tiles.shape[3], adj_tiles.shape[4]
    positions = node_perm.shape[1]
    w_chunk = width // 2 // parts
    vmem = pl.BlockSpec(memory_space=pltpu.VMEM)
    smem = pl.BlockSpec(memory_space=pltpu.SMEM)
    return pl.pallas_call(
        fused,
        out_shape=(
            jax.ShapeDtypeStruct((rows, width), BF16),
            jax.ShapeDtypeStruct((width, width), F32),
            jax.ShapeDtypeStruct((rows, width), BF16),
        ),
        in_specs=[vmem] * 4 + [pl.BlockSpec(memory_space=pl.ANY)] + [smem] * 3 + [vmem],
        out_specs=(vmem, vmem, vmem),
        scratch_shapes=[
            pltpu.VMEM((parts, rows, width), BF16),
            pltpu.VMEM((parts, slots, tile, tile), BF16),
            pltpu.VMEM((parts, positions, slots * tile), BF16),
            pltpu.VMEM((positions, tile), jnp.int32),
            pltpu.VMEM((2, rows, width), F32),
            pltpu.VMEM((rows, width), F32),
            pltpu.VMEM((rows, width), F32),
            pltpu.VMEM((2, parts, w_chunk, width), F32),
            pltpu.VMEM((parts, w_chunk, width), F32),
            pltpu.VMEM((parts, w_chunk, width), F32),
            pltpu.VMEM((parts, w_chunk, width), F32),
            pltpu.VMEM((parts, w_chunk, width), F32),
            pltpu.VMEM((parts, w_chunk, width), F32),
            pltpu.SemaphoreType.DMA,
            pltpu.SemaphoreType.DMA((LINE, 4)),
            pltpu.SemaphoreType.DMA((parts,)),
            pltpu.SemaphoreType.DMA((2, LINE)),
            pltpu.SemaphoreType.DMA((2, LINE)),
            pltpu.SemaphoreType.DMA((2, parts)),
            pltpu.SemaphoreType.DMA((2, parts)),
            pltpu.SemaphoreType.DMA((3,)),
            pltpu.SemaphoreType.DMA((3,)),
        ],
        compiler_params=pltpu.CompilerParams(
            collective_id=0, has_side_effects=True, vmem_limit_bytes=40 * 1024 * 1024
        ),
    )(
        grad_out,
        pre_act,
        aggregated,
        weight,
        adj_tiles.reshape(parts, slots, tile, tile),
        jnp.swapaxes(tile_row[0, 0], 0, 1),
        jnp.swapaxes(tile_col[0, 0], 0, 1),
        tile_count[0],
        node_perm,
    )


def tile_products(running, blocks, local_tiles, local_row, local_col, local_count):
    for slot in range(local_tiles.shape[1]):
        picked = local_row[:, slot][:, None, None]
        chosen = blocks[:, 0]
        for block in range(1, blocks.shape[1]):
            chosen = jnp.where(picked == block, blocks[:, block], chosen)
        product = jnp.einsum(
            "kab,kac->kbc", local_tiles[:, slot], chosen, preferred_element_type=F32
        )
        alive = (local_count > slot).astype(F32)
        running = running.at[local_col[:, slot]].add(product * alive[:, None, None])
    return running


def plain_body(
    grad_out, pre_act, aggregated, weight, adj_tiles, tile_row, tile_col, tile_count, node_perm
):
    row_count, feature_width = grad_out.shape[0], weight.shape[0]
    relu_grad = jnp.where(pre_act > 0, grad_out, jnp.zeros_like(grad_out))
    partial_weight = lax.dot_general(
        aggregated, relu_grad, (((0,), (0,)), ((), ())), preferred_element_type=F32
    )
    local_tiles = adj_tiles[0, 0]
    tile_size = local_tiles.shape[-1]
    row_blocks = row_count // tile_size
    col_blocks = lax.axis_size("rep") * row_blocks
    back_agg = lax.dot_general(
        relu_grad, weight, (((1,), (1,)), ((), ())), preferred_element_type=F32
    ).astype(BF16)
    sources = lax.all_gather(back_agg, "graph", axis=0, tiled=True)
    running = tile_products(
        jnp.zeros((col_blocks, tile_size, feature_width), F32),
        sources.reshape(-1, row_blocks, tile_size, feature_width),
        local_tiles,
        tile_row[0, 0],
        tile_col[0, 0],
        tile_count[0, 0],
    )
    partial_grad = running.reshape(col_blocks * tile_size, feature_width)
    input_grad = lax.psum_scatter(
        jnp.take(partial_grad, node_perm[0], axis=0), "rep", scatter_dimension=0, tiled=True
    ).astype(BF16)
    return (input_grad, lax.psum(partial_weight, ("graph", "rep")), relu_grad)


def solution(mesh):
    placed = (
        P(("graph", "rep"), None),
        P(("graph", "rep"), None),
        P(("graph", "rep"), None),
        P(),
        P("graph", "rep", None, None, None, None),
        P("graph", "rep", None, None),
        P("graph", "rep", None, None),
        P("graph", "rep", None),
        P("graph", None),
    )
    fits = mesh.shape["graph"] == LINE * PLANE and mesh.shape["rep"] == 2
    return jax.shard_map(
        fused_body if fits else plain_body,
        mesh=mesh,
        in_specs=placed,
        out_specs=(P(("graph", "rep"), None), P(), P(("graph", "rep"), None)),
        check_vma=False,
    )
```

```python
import functools

import jax
import jax.numpy as jnp
from jax import lax
from jax.experimental import pallas as pl
from jax.experimental.pallas import tpu as pltpu
from jax.sharding import PartitionSpec as P

MESH = pl.DeviceIdType.MESH
BF16 = jnp.bfloat16
F32 = jnp.float32
LINE = 4
PLANE = 4


def nearest(z, k):
    if k == 0:
        return z
    low = jnp.where(z < 2, z, 3 - z)
    value = (1 - low) if k == 1 else k
    return jnp.where(z < 2, value, 3 - value)


def fused(
    grad_hbm, pre_hbm, agg_hbm, weight_hbm, tiles_hbm, row_hbm, col_hbm, count_hbm, perm_hbm,
    input_hbm, wgrad_hbm, relu_hbm,
    input_ref, wgrad_ref, relu_ref, store_sem,
    grad_ref, pre_ref, agg_ref, weight_ref, row_ref, col_ref, count_ref, perm_ref, load_sem,
    blocks, tiles, folded, perm_wide, total, outgoing, incoming,
    w_part, w_pair, w_mine, w_parts, w_done, w_other,
    send_sem, recv_sem, diag_send, diag_recv, w_send, w_recv, pair_send, pair_recv,
):
    parts, rows, width = blocks.shape
    tile = tiles.shape[-1]
    g = lax.axis_index("graph")
    r = lax.axis_index("rep")
    other = 1 - r
    z = g // PLANE
    spot = g - z * PLANE
    y = spot // 2
    x = spot - y * 2
    across_y = (1 - y) * 2 + x
    across_x = y * 2 + (1 - x)
    across_xy = (1 - y) * 2 + (1 - x)

    def peer(k):
        return lax.rem(g + k, parts)

    loads = [
        pltpu.make_async_copy(src, dst, load_sem.at[i])
        for i, (src, dst) in enumerate((
            (grad_hbm, grad_ref), (pre_hbm, pre_ref), (weight_hbm, weight_ref), (agg_hbm, agg_ref),
            (perm_hbm, perm_ref), (count_hbm, count_ref), (col_hbm, col_ref), (row_hbm, row_ref),
            (tiles_hbm, tiles),
        ))
    ]
    for load in loads[:4]:
        load.start()

    store_input = pltpu.make_async_copy(input_ref, input_hbm, store_sem.at[0])
    store_wgrad = pltpu.make_async_copy(wgrad_ref, wgrad_hbm, store_sem.at[1])
    store_relu = pltpu.make_async_copy(relu_ref, relu_hbm, store_sem.at[2])

    barrier = pltpu.get_barrier_semaphore()

    def greet(k, carry):
        pl.semaphore_signal(barrier, inc=1, device_id=(peer(k), r), device_id_type=MESH)
        return carry

    lax.fori_loop(1, parts, greet, 0)
    pl.semaphore_signal(barrier, inc=1, device_id=(g, other), device_id_type=MESH)

    for load in loads[4:]:
        load.start()
    for load in loads[:3]:
        load.wait()

    grad = grad_ref[...]
    relu_ref[...] = jnp.where(pre_ref[...] > 0, grad, jnp.zeros_like(grad))
    blocks[g] = lax.dot_general(
        relu_ref[...], weight_ref[...], (((1,), (1,)), ((), ())), preferred_element_type=F32
    ).astype(BF16)

    def whole(origin, target, slot, way):
        return pltpu.make_async_remote_copy(
            src_ref=blocks.at[origin],
            dst_ref=blocks.at[origin],
            send_sem=send_sem.at[slot, way],
            recv_sem=recv_sem.at[origin],
            device_id=(target, r),
            device_id_type=MESH,
        )

    def half(k, via):
        zz = nearest(z, k)
        from_here = zz * PLANE + (across_y if via == 0 else across_x)
        part = pl.ds(via * tile, tile)
        return pltpu.make_async_remote_copy(
            src_ref=blocks.at[from_here, part],
            dst_ref=blocks.at[from_here, part],
            send_sem=diag_send.at[via, k],
            recv_sem=diag_recv.at[via, zz],
            device_id=(z * PLANE + (across_x if via == 0 else across_y), r),
            device_id_type=MESH,
        )

    def half_in(k, via):
        zz = nearest(z, k)
        origin = zz * PLANE + across_xy
        part = pl.ds(via * tile, tile)
        return pltpu.make_async_remote_copy(
            src_ref=blocks.at[origin, part],
            dst_ref=blocks.at[origin, part],
            send_sem=diag_send.at[via, k],
            recv_sem=diag_recv.at[via, zz],
            device_id=(z * PLANE + (across_x if via == 0 else across_y), r),
            device_id_type=MESH,
        )

    def along_z(k, act):
        zz = nearest(z, k)
        origin = zz * PLANE + spot
        if k == 0:
            @pl.when(z < LINE - 1)
            def _():
                act(whole(origin, g + PLANE, k, 0))

            @pl.when(z > 0)
            def _():
                act(whole(origin, g - PLANE, k, 1))
        else:
            @pl.when((zz < z) & (z < LINE - 1))
            def _():
                act(whole(origin, g + PLANE, k, 0))

            @pl.when((zz > z) & (z > 0))
            def _():
                act(whole(origin, g - PLANE, k, 1))

    def in_plane(k, act):
        origin = nearest(z, k) * PLANE + spot
        act(whole(origin, z * PLANE + across_y, k, 2))
        act(whole(origin, z * PLANE + across_x, k, 3))

    def start(copy):
        copy.start()

    def wait_sent(copy):
        copy.wait_send()

    def received(origin):
        whole(origin, z * PLANE + across_y, 0, 2).wait_recv()

    def spread(k):
        if k > 0:
            received(nearest(z, k) * PLANE + spot)
        along_z(k, start)
        in_plane(k, start)

    def turn(k):
        zz = nearest(z, k)
        received(zz * PLANE + across_y)
        half(k, 0).start()
        received(zz * PLANE + across_x)
        half(k, 1).start()

    def fold(first, many):
        lanes = lax.broadcasted_iota(jnp.int32, perm_wide.shape, 1)

        def one(p, carry):
            for s in range(2):
                base = jnp.where(count_ref[0, p] > s, col_ref[s, p] * tile, -4 * parts * rows)
                hot = jnp.where(perm_wide[...] == lanes + base, 1.0, 0.0).astype(BF16)
                folded[p, :, s * tile : (s + 1) * tile] = lax.dot_general(
                    hot, tiles[p, s], (((1,), (1,)), ((), ())), preferred_element_type=F32
                ).astype(BF16)
            return carry

        lax.fori_loop(first, first + many, one, 0)

    def chosen(p):
        top = blocks[p, :tile, :]
        low = blocks[p, tile:, :]
        return jnp.concatenate([jnp.where(row_ref[s, p] == 0, top, low) for s in range(2)], axis=0)

    def product(p, side, source):
        return jnp.dot(
            folded[p, pl.ds(side * rows, rows), :], source, preferred_element_type=F32
        )

    def add(p, first=False):
        source = chosen(p)
        for side in range(2):
            if first:
                total[side] = product(p, side, source)
            else:
                total[side] += product(p, side, source)

    def pair(src, dst, which):
        return pltpu.make_async_remote_copy(
            src_ref=src,
            dst_ref=dst,
            send_sem=pair_send.at[which],
            recv_sem=pair_recv.at[which],
            device_id=(g, other),
            device_id_type=MESH,
        )

    def scatter_w(k):
        to = peer(k)
        return pltpu.make_async_remote_copy(
            src_ref=w_mine.at[to],
            dst_ref=w_parts.at[g],
            send_sem=w_send.at[0, k],
            recv_sem=w_recv.at[0, g],
            device_id=(to, r),
            device_id_type=MESH,
        )

    def gather_w(k):
        return pltpu.make_async_remote_copy(
            src_ref=w_done.at[g],
            dst_ref=w_done.at[g],
            send_sem=w_send.at[1, k],
            recv_sem=w_recv.at[1, g],
            device_id=(peer(k), r),
            device_id_type=MESH,
        )

    def wait_w(phase, buffer):
        def one(k, carry):
            origin = peer(k)
            pltpu.make_async_remote_copy(
                src_ref=buffer.at[origin],
                dst_ref=buffer.at[origin],
                send_sem=w_send.at[phase, k],
                recv_sem=w_recv.at[phase, origin],
                device_id=(origin, r),
                device_id_type=MESH,
            ).wait_recv()
            return carry

        lax.fori_loop(1, parts, one, 0)

    def each_peer(make, act):
        def one(k, carry):
            act(make(k))
            return carry

        lax.fori_loop(1, parts, one, 0)

    pl.semaphore_wait(barrier, parts)
    spread(0)
    store_relu.start()

    for load in loads[3:]:
        load.wait()
    w_part[...] = lax.dot_general(
        agg_ref[...], relu_ref[...], (((0,), (0,)), ((), ())), preferred_element_type=F32
    ).reshape(w_part.shape)
    w_swap = pair(w_part.at[other], w_pair, 0)
    w_swap.start()

    perm_wide[...] = jnp.broadcast_to(perm_ref[...], (tile, perm_wide.shape[0])).T
    fold(0, 2)
    spread(1)

    w_swap.wait_recv()
    w_mine[...] = w_part[r] + w_pair[...]
    each_peer(scatter_w, start)
    w_parts[g] = w_mine[g]
    turn(0)
    fold(2, 4)
    spread(2)
    turn(1)
    wait_w(0, w_parts)
    w_done[g] = jnp.sum(w_parts[...], axis=0)
    each_peer(gather_w, start)
    fold(6, 4)
    spread(3)
    turn(2)
    fold(10, 6)
    turn(3)
    wait_w(1, w_done)
    w_back = pair(w_done, w_other, 1)
    w_back.start()

    add(g, first=True)
    for k in range(1, LINE):
        add(nearest(z, k) * PLANE + spot)
    for k in range(LINE):
        add(nearest(z, k) * PLANE + across_y)
        add(nearest(z, k) * PLANE + across_x)

    w_back.wait_recv()
    w_rows = width // 2
    wgrad_ref[pl.ds(pl.multiple_of(r * w_rows, w_rows), w_rows), :] = w_done[...].reshape(w_rows, width)
    wgrad_ref[pl.ds(pl.multiple_of(other * w_rows, w_rows), w_rows), :] = w_other[...].reshape(w_rows, width)
    store_wgrad.start()

    for k in range(LINE):
        half_in(k, 0).wait_recv()
        half_in(k, 1).wait_recv()
        p = nearest(z, k) * PLANE + across_xy
        if k < LINE - 1:
            add(p)
    source = chosen(p)
    outgoing[...] = total[other] + product(p, other, source)
    swap = pair(outgoing, incoming, 2)
    swap.start()
    total[r] += product(p, r, source)

    for k in range(LINE):
        along_z(k, wait_sent)
        in_plane(k, wait_sent)
        half(k, 0).wait_send()
        half(k, 1).wait_send()
    each_peer(scatter_w, wait_sent)
    each_peer(gather_w, wait_sent)
    w_swap.wait_send()
    w_back.wait_send()
    swap.wait_recv()
    input_ref[...] = (total[r] + incoming[...]).astype(BF16)
    store_input.start()
    swap.wait_send()
    store_relu.wait()
    store_wgrad.wait()
    store_input.wait()


def write_out(*refs):
    copies = [
        pltpu.make_async_copy(refs[i], refs[3 + i], refs[6].at[i]) for i in range(3)
    ]
    for copy in copies:
        copy.start()
    for copy in copies:
        copy.wait()


def fused_body(
    grad_out, pre_act, aggregated, weight, adj_tiles, tile_row, tile_col, tile_count, node_perm
):
    rows, width = grad_out.shape
    parts, slots, tile = adj_tiles.shape[2], adj_tiles.shape[3], adj_tiles.shape[4]
    positions = node_perm.shape[1]
    w_chunk = width // 2 // parts
    anywhere = pl.BlockSpec(memory_space=pl.ANY)
    hbm = pl.BlockSpec(memory_space=pltpu.HBM)
    results = (
        jax.ShapeDtypeStruct((rows, width), BF16),
        jax.ShapeDtypeStruct((width, width), F32),
        jax.ShapeDtypeStruct((rows, width), BF16),
    )
    made = pl.pallas_call(
        fused,
        out_shape=results,
        in_specs=[hbm] * 9,
        out_specs=(hbm, hbm, hbm),
        scratch_shapes=[
            pltpu.VMEM((rows, width), BF16),
            pltpu.VMEM((width, width), F32),
            pltpu.VMEM((rows, width), BF16),
            pltpu.SemaphoreType.DMA((3,)),
            pltpu.VMEM((rows, width), BF16),
            pltpu.VMEM((rows, width), BF16),
            pltpu.VMEM((rows, width), BF16),
            pltpu.VMEM((width, width), BF16),
            pltpu.SMEM((slots, parts), jnp.int32),
            pltpu.SMEM((slots, parts), jnp.int32),
            pltpu.SMEM((1, parts), jnp.int32),
            pltpu.VMEM((1, positions), jnp.int32),
            pltpu.SemaphoreType.DMA((9,)),
            pltpu.VMEM((parts, rows, width), BF16),
            pltpu.VMEM((parts, slots, tile, tile), BF16),
            pltpu.VMEM((parts, positions, slots * tile), BF16),
            pltpu.VMEM((positions, tile), jnp.int32),
            pltpu.VMEM((2, rows, width), F32),
            pltpu.VMEM((rows, width), F32),
            pltpu.VMEM((rows, width), F32),
            pltpu.VMEM((2, parts, w_chunk, width), F32),
            pltpu.VMEM((parts, w_chunk, width), F32),
            pltpu.VMEM((parts, w_chunk, width), F32),
            pltpu.VMEM((parts, w_chunk, width), F32),
            pltpu.VMEM((parts, w_chunk, width), F32),
            pltpu.VMEM((parts, w_chunk, width), F32),
            pltpu.SemaphoreType.DMA((LINE, 4)),
            pltpu.SemaphoreType.DMA((parts,)),
            pltpu.SemaphoreType.DMA((2, LINE)),
            pltpu.SemaphoreType.DMA((2, LINE)),
            pltpu.SemaphoreType.DMA((2, parts)),
            pltpu.SemaphoreType.DMA((2, parts)),
            pltpu.SemaphoreType.DMA((3,)),
            pltpu.SemaphoreType.DMA((3,)),
        ],
        compiler_params=pltpu.CompilerParams(
            collective_id=0, has_side_effects=True, vmem_limit_bytes=60 * 1024 * 1024
        ),
    )(
        grad_out,
        pre_act,
        aggregated,
        weight,
        adj_tiles.reshape(parts, slots, tile, tile),
        jnp.swapaxes(tile_row[0, 0], 0, 1),
        jnp.swapaxes(tile_col[0, 0], 0, 1),
        tile_count[0],
        node_perm,
    )
    return pl.pallas_call(
        write_out,
        out_shape=results,
        in_specs=[anywhere] * 3,
        out_specs=(hbm, hbm, hbm),
        scratch_shapes=[pltpu.SemaphoreType.DMA((3,))],
        compiler_params=pltpu.CompilerParams(vmem_limit_bytes=60 * 1024 * 1024),
    )(*made)


def tile_products(running, blocks, local_tiles, local_row, local_col, local_count):
    for slot in range(local_tiles.shape[1]):
        picked = local_row[:, slot][:, None, None]
        chosen = blocks[:, 0]
        for block in range(1, blocks.shape[1]):
            chosen = jnp.where(picked == block, blocks[:, block], chosen)
        product = jnp.einsum(
            "kab,kac->kbc", local_tiles[:, slot], chosen, preferred_element_type=F32
        )
        alive = (local_count > slot).astype(F32)
        running = running.at[local_col[:, slot]].add(product * alive[:, None, None])
    return running


def plain_body(
    grad_out, pre_act, aggregated, weight, adj_tiles, tile_row, tile_col, tile_count, node_perm
):
    row_count, feature_width = grad_out.shape[0], weight.shape[0]
    relu_grad = jnp.where(pre_act > 0, grad_out, jnp.zeros_like(grad_out))
    partial_weight = lax.dot_general(
        aggregated, relu_grad, (((0,), (0,)), ((), ())), preferred_element_type=F32
    )
    local_tiles = adj_tiles[0, 0]
    tile_size = local_tiles.shape[-1]
    row_blocks = row_count // tile_size
    col_blocks = lax.axis_size("rep") * row_blocks
    back_agg = lax.dot_general(
        relu_grad, weight, (((1,), (1,)), ((), ())), preferred_element_type=F32
    ).astype(BF16)
    sources = lax.all_gather(back_agg, "graph", axis=0, tiled=True)
    running = tile_products(
        jnp.zeros((col_blocks, tile_size, feature_width), F32),
        sources.reshape(-1, row_blocks, tile_size, feature_width),
        local_tiles,
        tile_row[0, 0],
        tile_col[0, 0],
        tile_count[0, 0],
    )
    partial_grad = running.reshape(col_blocks * tile_size, feature_width)
    input_grad = lax.psum_scatter(
        jnp.take(partial_grad, node_perm[0], axis=0), "rep", scatter_dimension=0, tiled=True
    ).astype(BF16)
    return (input_grad, lax.psum(partial_weight, ("graph", "rep")), relu_grad)


def solution(mesh):
    placed = (
        P(("graph", "rep"), None),
        P(("graph", "rep"), None),
        P(("graph", "rep"), None),
        P(),
        P("graph", "rep", None, None, None, None),
        P("graph", "rep", None, None),
        P("graph", "rep", None, None),
        P("graph", "rep", None),
        P("graph", None),
    )
    fits = mesh.shape["graph"] == LINE * PLANE and mesh.shape["rep"] == 2
    return jax.shard_map(
        fused_body if fits else plain_body,
        mesh=mesh,
        in_specs=placed,
        out_specs=(P(("graph", "rep"), None), P(), P(("graph", "rep"), None)),
        check_vma=False,
    )
```

```python
import functools

import jax
import jax.numpy as jnp
from jax import lax
from jax.experimental import pallas as pl
from jax.experimental.pallas import tpu as pltpu
from jax.sharding import PartitionSpec as P

MESH = pl.DeviceIdType.MESH
BF16 = jnp.bfloat16
F32 = jnp.float32
LINE = 4
PLANE = 4


def nearest(z, k):
    if k == 0:
        return z
    low = jnp.where(z < 2, z, 3 - z)
    value = (1 - low) if k == 1 else k
    return jnp.where(z < 2, value, 3 - value)


def fused(
    grad_hbm, pre_hbm, agg_hbm, weight_hbm, tiles_hbm, row_hbm, col_hbm, count_hbm, perm_hbm,
    input_hbm, wgrad_hbm, relu_hbm,
    input_ref, wgrad_ref, relu_ref, store_sem,
    grad_ref, pre_ref, agg_ref, weight_ref, row_ref, col_ref, count_ref, perm_ref, load_sem,
    blocks, tiles, folded, perm_wide, total, outgoing, incoming,
    w_part, w_pair, w_mine, w_parts, w_done, w_other,
    send_sem, recv_sem, diag_send, diag_recv, w_send, w_recv, pair_send, pair_recv,
):
    parts, rows, width = blocks.shape
    tile = tiles.shape[-1]
    g = lax.axis_index("graph")
    r = lax.axis_index("rep")
    other = 1 - r
    z = g // PLANE
    spot = g - z * PLANE
    y = spot // 2
    x = spot - y * 2
    across_y = (1 - y) * 2 + x
    across_x = y * 2 + (1 - x)
    across_xy = (1 - y) * 2 + (1 - x)

    def peer(k):
        return lax.rem(g + k, parts)

    loads = [
        pltpu.make_async_copy(src, dst, load_sem.at[i])
        for i, (src, dst) in enumerate((
            (grad_hbm, grad_ref), (pre_hbm, pre_ref), (weight_hbm, weight_ref), (agg_hbm, agg_ref),
            (perm_hbm, perm_ref), (count_hbm, count_ref), (col_hbm, col_ref), (row_hbm, row_ref),
            (tiles_hbm, tiles),
        ))
    ]
    for load in loads[:4]:
        load.start()

    store_input = pltpu.make_async_copy(input_ref, input_hbm, store_sem.at[0])
    store_wgrad = pltpu.make_async_copy(wgrad_ref, wgrad_hbm, store_sem.at[1])
    store_relu = pltpu.make_async_copy(relu_ref, relu_hbm, store_sem.at[2])

    barrier = pltpu.get_barrier_semaphore()

    def greet(k, carry):
        pl.semaphore_signal(barrier, inc=1, device_id=(peer(k), r), device_id_type=MESH)
        return carry

    lax.fori_loop(1, parts, greet, 0)
    pl.semaphore_signal(barrier, inc=1, device_id=(g, other), device_id_type=MESH)

    for load in loads[4:]:
        load.start()
    for load in loads[:3]:
        load.wait()

    grad = grad_ref[...]
    relu_ref[...] = jnp.where(pre_ref[...] > 0, grad, jnp.zeros_like(grad))
    blocks[g] = lax.dot_general(
        relu_ref[...], weight_ref[...], (((1,), (1,)), ((), ())), preferred_element_type=F32
    ).astype(BF16)

    def whole(origin, target, slot, way):
        return pltpu.make_async_remote_copy(
            src_ref=blocks.at[origin],
            dst_ref=blocks.at[origin],
            send_sem=send_sem.at[slot, way],
            recv_sem=recv_sem.at[origin],
            device_id=(target, r),
            device_id_type=MESH,
        )

    def half(k, via):
        zz = nearest(z, k)
        from_here = zz * PLANE + (across_y if via == 0 else across_x)
        part = pl.ds(via * tile, tile)
        return pltpu.make_async_remote_copy(
            src_ref=blocks.at[from_here, part],
            dst_ref=blocks.at[from_here, part],
            send_sem=diag_send.at[via, k],
            recv_sem=diag_recv.at[via, zz],
            device_id=(z * PLANE + (across_x if via == 0 else across_y), r),
            device_id_type=MESH,
        )

    def half_in(k, via):
        zz = nearest(z, k)
        origin = zz * PLANE + across_xy
        part = pl.ds(via * tile, tile)
        return pltpu.make_async_remote_copy(
            src_ref=blocks.at[origin, part],
            dst_ref=blocks.at[origin, part],
            send_sem=diag_send.at[via, k],
            recv_sem=diag_recv.at[via, zz],
            device_id=(z * PLANE + (across_x if via == 0 else across_y), r),
            device_id_type=MESH,
        )

    def along_z(k, act):
        zz = nearest(z, k)
        origin = zz * PLANE + spot
        if k == 0:
            @pl.when(z < LINE - 1)
            def _():
                act(whole(origin, g + PLANE, k, 0))

            @pl.when(z > 0)
            def _():
                act(whole(origin, g - PLANE, k, 1))
        else:
            @pl.when((zz < z) & (z < LINE - 1))
            def _():
                act(whole(origin, g + PLANE, k, 0))

            @pl.when((zz > z) & (z > 0))
            def _():
                act(whole(origin, g - PLANE, k, 1))

    def in_plane(k, act):
        origin = nearest(z, k) * PLANE + spot
        act(whole(origin, z * PLANE + across_y, k, 2))
        act(whole(origin, z * PLANE + across_x, k, 3))

    def start(copy):
        copy.start()

    def wait_sent(copy):
        copy.wait_send()

    def received(origin):
        whole(origin, z * PLANE + across_y, 0, 2).wait_recv()

    def spread(k):
        if k > 0:
            received(nearest(z, k) * PLANE + spot)
        along_z(k, start)
        in_plane(k, start)

    def turn(k):
        zz = nearest(z, k)
        received(zz * PLANE + across_y)
        half(k, 0).start()
        received(zz * PLANE + across_x)
        half(k, 1).start()

    def fold(first, many):
        lanes = lax.broadcasted_iota(jnp.int32, perm_wide.shape, 1)

        def one(p, carry):
            for s in range(2):
                base = jnp.where(count_ref[0, p] > s, col_ref[s, p] * tile, -4 * parts * rows)
                hot = jnp.where(perm_wide[...] == lanes + base, 1.0, 0.0).astype(BF16)
                folded[p, :, s * tile : (s + 1) * tile] = lax.dot_general(
                    hot, tiles[p, s], (((1,), (1,)), ((), ())), preferred_element_type=F32
                ).astype(BF16)
            return carry

        lax.fori_loop(first, first + many, one, 0)

    def chosen(p):
        top = blocks[p, :tile, :]
        low = blocks[p, tile:, :]
        return jnp.concatenate([jnp.where(row_ref[s, p] == 0, top, low) for s in range(2)], axis=0)

    def product(p, side, source):
        return jnp.dot(
            folded[p, pl.ds(side * rows, rows), :], source, preferred_element_type=F32
        )

    def add(p, first=False):
        source = chosen(p)
        for side in range(2):
            if first:
                total[side] = product(p, side, source)
            else:
                total[side] += product(p, side, source)

    def pair(src, dst, which):
        return pltpu.make_async_remote_copy(
            src_ref=src,
            dst_ref=dst,
            send_sem=pair_send.at[which],
            recv_sem=pair_recv.at[which],
            device_id=(g, other),
            device_id_type=MESH,
        )

    def scatter_w(k):
        to = peer(k)
        return pltpu.make_async_remote_copy(
            src_ref=w_mine.at[to],
            dst_ref=w_parts.at[g],
            send_sem=w_send.at[0, k],
            recv_sem=w_recv.at[0, g],
            device_id=(to, r),
            device_id_type=MESH,
        )

    def gather_w(k):
        return pltpu.make_async_remote_copy(
            src_ref=w_done.at[g],
            dst_ref=w_done.at[g],
            send_sem=w_send.at[1, k],
            recv_sem=w_recv.at[1, g],
            device_id=(peer(k), r),
            device_id_type=MESH,
        )

    def wait_w(phase, buffer):
        def one(k, carry):
            origin = peer(k)
            pltpu.make_async_remote_copy(
                src_ref=buffer.at[origin],
                dst_ref=buffer.at[origin],
                send_sem=w_send.at[phase, k],
                recv_sem=w_recv.at[phase, origin],
                device_id=(origin, r),
                device_id_type=MESH,
            ).wait_recv()
            return carry

        lax.fori_loop(1, parts, one, 0)

    def each_peer(make, act):
        def one(k, carry):
            act(make(k))
            return carry

        lax.fori_loop(1, parts, one, 0)

    pl.semaphore_wait(barrier, parts)
    spread(0)
    store_relu.start()

    for load in loads[3:]:
        load.wait()
    w_part[...] = lax.dot_general(
        agg_ref[...], relu_ref[...], (((0,), (0,)), ((), ())), preferred_element_type=F32
    ).reshape(w_part.shape)
    w_swap = pair(w_part.at[other], w_pair, 0)
    w_swap.start()

    perm_wide[...] = jnp.broadcast_to(perm_ref[...], (tile, perm_wide.shape[0])).T
    fold(0, 2)
    spread(1)

    w_swap.wait_recv()
    w_mine[...] = w_part[r] + w_pair[...]
    each_peer(scatter_w, start)
    w_parts[g] = w_mine[g]
    turn(0)
    fold(2, 4)
    spread(2)
    turn(1)
    wait_w(0, w_parts)
    w_done[g] = jnp.sum(w_parts[...], axis=0)
    each_peer(gather_w, start)
    fold(6, 4)
    spread(3)
    turn(2)
    fold(10, 6)
    turn(3)
    wait_w(1, w_done)
    w_back = pair(w_done, w_other, 1)
    w_back.start()

    add(g, first=True)
    for k in range(1, LINE):
        add(nearest(z, k) * PLANE + spot)
    for k in range(LINE):
        add(nearest(z, k) * PLANE + across_y)
        add(nearest(z, k) * PLANE + across_x)

    w_back.wait_recv()
    w_rows = width // 2
    wgrad_ref[pl.ds(pl.multiple_of(r * w_rows, w_rows), w_rows), :] = w_done[...].reshape(w_rows, width)
    wgrad_ref[pl.ds(pl.multiple_of(other * w_rows, w_rows), w_rows), :] = w_other[...].reshape(w_rows, width)
    store_wgrad.start()

    for k in range(LINE):
        half_in(k, 0).wait_recv()
        half_in(k, 1).wait_recv()
        p = nearest(z, k) * PLANE + across_xy
        if k < LINE - 1:
            add(p)
    source = chosen(p)
    outgoing[...] = total[other] + product(p, other, source)
    swap = pair(outgoing, incoming, 2)
    swap.start()
    total[r] += product(p, r, source)

    for k in range(LINE):
        along_z(k, wait_sent)
        in_plane(k, wait_sent)
        half(k, 0).wait_send()
        half(k, 1).wait_send()
    each_peer(scatter_w, wait_sent)
    each_peer(gather_w, wait_sent)
    w_swap.wait_send()
    w_back.wait_send()
    swap.wait_recv()
    input_ref[...] = (total[r] + incoming[...]).astype(BF16)
    store_input.start()
    swap.wait_send()
    store_relu.wait()
    store_wgrad.wait()
    store_input.wait()


def write_out(*refs):
    made, results, held, sems = refs[:3], refs[3:6], refs[6:9], refs[9]
    reads = [pltpu.make_async_copy(made[i], held[i], sems.at[0, i]) for i in range(3)]
    writes = [pltpu.make_async_copy(held[i], results[i], sems.at[1, i]) for i in range(3)]
    for read in reads:
        read.start()
    for read, write in zip(reads, writes):
        read.wait()
        write.start()
    for write in writes:
        write.wait()


def fused_body(
    grad_out, pre_act, aggregated, weight, adj_tiles, tile_row, tile_col, tile_count, node_perm
):
    rows, width = grad_out.shape
    parts, slots, tile = adj_tiles.shape[2], adj_tiles.shape[3], adj_tiles.shape[4]
    positions = node_perm.shape[1]
    w_chunk = width // 2 // parts
    anywhere = pl.BlockSpec(memory_space=pl.ANY)
    hbm = pl.BlockSpec(memory_space=pltpu.HBM)
    results = (
        jax.ShapeDtypeStruct((rows, width), BF16),
        jax.ShapeDtypeStruct((width, width), F32),
        jax.ShapeDtypeStruct((rows, width), BF16),
    )
    made = pl.pallas_call(
        fused,
        out_shape=results,
        in_specs=[hbm] * 9,
        out_specs=(hbm, hbm, hbm),
        scratch_shapes=[
            pltpu.VMEM((rows, width), BF16),
            pltpu.VMEM((width, width), F32),
            pltpu.VMEM((rows, width), BF16),
            pltpu.SemaphoreType.DMA((3,)),
            pltpu.VMEM((rows, width), BF16),
            pltpu.VMEM((rows, width), BF16),
            pltpu.VMEM((rows, width), BF16),
            pltpu.VMEM((width, width), BF16),
            pltpu.SMEM((slots, parts), jnp.int32),
            pltpu.SMEM((slots, parts), jnp.int32),
            pltpu.SMEM((1, parts), jnp.int32),
            pltpu.VMEM((1, positions), jnp.int32),
            pltpu.SemaphoreType.DMA((9,)),
            pltpu.VMEM((parts, rows, width), BF16),
            pltpu.VMEM((parts, slots, tile, tile), BF16),
            pltpu.VMEM((parts, positions, slots * tile), BF16),
            pltpu.VMEM((positions, tile), jnp.int32),
            pltpu.VMEM((2, rows, width), F32),
            pltpu.VMEM((rows, width), F32),
            pltpu.VMEM((rows, width), F32),
            pltpu.VMEM((2, parts, w_chunk, width), F32),
            pltpu.VMEM((parts, w_chunk, width), F32),
            pltpu.VMEM((parts, w_chunk, width), F32),
            pltpu.VMEM((parts, w_chunk, width), F32),
            pltpu.VMEM((parts, w_chunk, width), F32),
            pltpu.VMEM((parts, w_chunk, width), F32),
            pltpu.SemaphoreType.DMA((LINE, 4)),
            pltpu.SemaphoreType.DMA((parts,)),
            pltpu.SemaphoreType.DMA((2, LINE)),
            pltpu.SemaphoreType.DMA((2, LINE)),
            pltpu.SemaphoreType.DMA((2, parts)),
            pltpu.SemaphoreType.DMA((2, parts)),
            pltpu.SemaphoreType.DMA((3,)),
            pltpu.SemaphoreType.DMA((3,)),
        ],
        compiler_params=pltpu.CompilerParams(
            collective_id=0, has_side_effects=True, vmem_limit_bytes=60 * 1024 * 1024
        ),
    )(
        grad_out,
        pre_act,
        aggregated,
        weight,
        adj_tiles.reshape(parts, slots, tile, tile),
        jnp.swapaxes(tile_row[0, 0], 0, 1),
        jnp.swapaxes(tile_col[0, 0], 0, 1),
        tile_count[0],
        node_perm,
    )
    return pl.pallas_call(
        write_out,
        out_shape=results,
        in_specs=[anywhere] * 3,
        out_specs=(hbm, hbm, hbm),
        scratch_shapes=[pltpu.VMEM(made_one.shape, made_one.dtype) for made_one in results]
        + [pltpu.SemaphoreType.DMA((2, 3))],
        compiler_params=pltpu.CompilerParams(vmem_limit_bytes=60 * 1024 * 1024),
    )(*made)


def tile_products(running, blocks, local_tiles, local_row, local_col, local_count):
    for slot in range(local_tiles.shape[1]):
        picked = local_row[:, slot][:, None, None]
        chosen = blocks[:, 0]
        for block in range(1, blocks.shape[1]):
            chosen = jnp.where(picked == block, blocks[:, block], chosen)
        product = jnp.einsum(
            "kab,kac->kbc", local_tiles[:, slot], chosen, preferred_element_type=F32
        )
        alive = (local_count > slot).astype(F32)
        running = running.at[local_col[:, slot]].add(product * alive[:, None, None])
    return running


def plain_body(
    grad_out, pre_act, aggregated, weight, adj_tiles, tile_row, tile_col, tile_count, node_perm
):
    row_count, feature_width = grad_out.shape[0], weight.shape[0]
    relu_grad = jnp.where(pre_act > 0, grad_out, jnp.zeros_like(grad_out))
    partial_weight = lax.dot_general(
        aggregated, relu_grad, (((0,), (0,)), ((), ())), preferred_element_type=F32
    )
    local_tiles = adj_tiles[0, 0]
    tile_size = local_tiles.shape[-1]
    row_blocks = row_count // tile_size
    col_blocks = lax.axis_size("rep") * row_blocks
    back_agg = lax.dot_general(
        relu_grad, weight, (((1,), (1,)), ((), ())), preferred_element_type=F32
    ).astype(BF16)
    sources = lax.all_gather(back_agg, "graph", axis=0, tiled=True)
    running = tile_products(
        jnp.zeros((col_blocks, tile_size, feature_width), F32),
        sources.reshape(-1, row_blocks, tile_size, feature_width),
        local_tiles,
        tile_row[0, 0],
        tile_col[0, 0],
        tile_count[0, 0],
    )
    partial_grad = running.reshape(col_blocks * tile_size, feature_width)
    input_grad = lax.psum_scatter(
        jnp.take(partial_grad, node_perm[0], axis=0), "rep", scatter_dimension=0, tiled=True
    ).astype(BF16)
    return (input_grad, lax.psum(partial_weight, ("graph", "rep")), relu_grad)


def solution(mesh):
    placed = (
        P(("graph", "rep"), None),
        P(("graph", "rep"), None),
        P(("graph", "rep"), None),
        P(),
        P("graph", "rep", None, None, None, None),
        P("graph", "rep", None, None),
        P("graph", "rep", None, None),
        P("graph", "rep", None),
        P("graph", None),
    )
    fits = mesh.shape["graph"] == LINE * PLANE and mesh.shape["rep"] == 2
    return jax.shard_map(
        fused_body if fits else plain_body,
        mesh=mesh,
        in_specs=placed,
        out_specs=(P(("graph", "rep"), None), P(), P(("graph", "rep"), None)),
        check_vma=False,
    )
```
